768 devices in a mesh: blk: 48 (over x, z_lo, core), narrow: 16 (over y, z_hi).
Axes of the slice: x: 4, y: 8, z: 12 (z_hi: 2, z_lo: 6; z = z_hi * 6 + z_lo), core: 2. Of those that a mesh axis runs over, the one named last changes fastest.
Arguments:
- picture_vectors: bfloat16 [196608, 1152], P(('blk', 'narrow')), may hold values from -0.1875 to 0.1875
- caption_vectors: bfloat16 [196608, 1152], P('blk', 'narrow'), may hold values from -0.1875 to 0.1875
- sharpness_weight: float32 [1], replicated, may hold values from 4 to 16
- score_offset_term: float32 [1], replicated, may hold values from -5 to -1
Outputs:
- pair_loss: float32 [196608], P(('blk', 'narrow'))
- image_grad: float32 [196608, 1152], P(('blk', 'narrow'))
- text_grad: float32 [196608, 1152], P('blk', 'narrow')
The draws below stay inside these ranges and needn't reach their ends.
All inputs are finite; a program needn't handle non-finite values.
Results may differ from the reference program's by a relative error of at most 0.0039.
Values may be sent and summed in bfloat16 or wider, within the bound.
A program may use at most 32 MiB of HBM per device.

```python
import math
import jax
import jax.numpy as jnp
from jax import lax

D = 1152
ROWS = 256
PAIRS = 196608
N_BLK = 48
N_NARROW = 16


def steps_of(key, dims, cuts, least, top_value):
    gain, own = 1.0, jax.random.fold_in(key, 6)
    for axis_at, shards_of in cuts:
        heights = jnp.exp(jax.random.uniform(jax.random.fold_in(own, axis_at), (shards_of,), jnp.float32, least / len(cuts), top_value / len(cuts)))
        gain = gain * jnp.repeat(heights, dims[axis_at] // shards_of).reshape([-1 if axis == axis_at else 1 for axis in range(len(dims))])
    return gain


def bell_draw(rng, shape, spread, reach, cuts=(), kind=jnp.bfloat16):
    result = spread * jax.random.normal(rng, shape, jnp.float32)
    if cuts:
        result = result * steps_of(rng, shape, cuts, -0.22, 0.18)
    return jnp.clip(result, -reach, reach).astype(kind)


def setup_inputs(seed: int = 0) -> dict:
    arg_keys = jax.random.split(jax.random.key(seed), 5)
    return {
        "picture_vectors": bell_draw(arg_keys[0], (PAIRS, D), D ** -0.5, 0.1875, ((0, 768),)),
        "caption_vectors": bell_draw(arg_keys[1], (PAIRS, D), D ** -0.5, 0.1875, ((0, 48), (1, 16))),
        "sharpness_weight": jnp.clip(jnp.exp(jax.random.uniform(arg_keys[2], (1,), jnp.float32, math.log(4.0), math.log(16.0))), 4.0, 16.0),
        "score_offset_term": jnp.clip(jax.random.uniform(arg_keys[3], (1,), jnp.float32, -5.0, -1.0), -5.0, -1.0),
    }


EPS = 1e-06

def unit_rows(values):
    full = values.astype(jnp.float32)
    norms = jnp.sqrt(lax.optimization_barrier(jnp.sum(full * full, axis=-1, keepdims=True)) + EPS)
    return (full / norms, norms)

def returned_rows(units, norms, direction_derivative):
    inner = lax.optimization_barrier(jnp.sum(units * direction_derivative, axis=-1, keepdims=True))
    return (direction_derivative - units * inner) / norms

def lowered(values):
    return lax.optimization_barrier(values.astype(jnp.bfloat16)).astype(jnp.float32)

def reference(picture_vectors, caption_vectors, sharpness_weight, score_offset_term):
    image_unit, image_norm = unit_rows(picture_vectors)
    unit_text_embed, text_norm = unit_rows(caption_vectors)
    shape4 = (N_BLK, N_NARROW, ROWS, D)
    image_low = lowered(image_unit).reshape(shape4)
    text_low = lowered(unit_text_embed).reshape(shape4)
    sharpness_factor = sharpness_weight[0]
    offset = score_offset_term[0]
    ident = jnp.eye(ROWS, dtype=jnp.float32)
    loss = jnp.zeros((N_BLK, N_NARROW, ROWS), jnp.float32)
    image_acc = jnp.zeros(shape4, jnp.float32)
    text_acc = jnp.zeros(shape4, jnp.float32)
    for step in (-1, 0, 1):
        window = jnp.roll(text_low, -step, axis=0)
        pair_logits = sharpness_factor * jnp.einsum('bnkd,bnjd->bnkj', image_low, window) + offset
        positive = ident if step == 0 else jnp.zeros_like(ident)
        loss = loss + lax.optimization_barrier(jnp.sum(jax.nn.softplus((1.0 - 2.0 * positive) * pair_logits), axis=-1))
        coef = lowered(sharpness_factor * (jax.nn.sigmoid(pair_logits) - positive))
        image_acc = image_acc + jnp.einsum('bnkj,bnjd->bnkd', coef, window)
        partial_sum = jnp.einsum('bnkj,bnkd->bnjd', coef, image_low)
        text_acc = text_acc + jnp.roll(partial_sum, step, axis=0)
    image_grad = returned_rows(image_unit, image_norm, image_acc.reshape(PAIRS, D))
    text_grad = returned_rows(unit_text_embed, text_norm, text_acc.reshape(PAIRS, D))
    return (loss.reshape(PAIRS), image_grad, text_grad)
```

```python
import functools

import jax
import jax.numpy as jnp
from jax import lax
from jax.experimental import pallas as pl
from jax.experimental.pallas import tpu as pltpu
from jax.sharding import PartitionSpec as P

EPS = 1e-06
MESH = pl.DeviceIdType.MESH
F32, BF16 = jnp.float32, jnp.bfloat16


def fold(chunk):
    half = chunk.shape[1] // 2
    return jnp.concatenate([chunk[:, :half], chunk[:, half:]], axis=0)


def unfold(chunk):
    cols = chunk.shape[0] // 2
    return jnp.concatenate([chunk[:cols], chunk[cols:]], axis=1)


def dot(left, right, contract):
    return lax.dot_general(left, right, ((contract[:1], contract[1:]), ((), ())), preferred_element_type=F32)


def softplus(x):
    return jnp.maximum(x, 0.0) + jnp.log1p(jnp.exp(-jnp.abs(x)))


def kernel(
    n_blk, n_narrow,
    pic_ref, cap_ref, sharp_ref, offset_ref,
    loss_ref, image_grad_ref, text_grad_ref,
    image_low, image_turned, packed, got, raw, text_low, back_out, back_in,
    pack_sent, pack_got, image_sent, image_got, text_sent, text_got, back_sent, back_got,
):
    b, n = lax.axis_index("blk"), lax.axis_index("narrow")
    rows, depth = pic_ref.shape
    cols = depth // n_narrow
    above, below = lax.rem(b + 1, n_blk), lax.rem(b + n_blk - 1, n_blk)
    far = 1 - lax.rem(n, 2)

    def peer(k):
        side = jnp.where(k < n_narrow // 2, far, 1 - far)
        step = lax.rem(k + 1, n_narrow // 2)
        return lax.rem(n // 2 + step, n_narrow // 2) * 2 + side

    barrier = pltpu.get_barrier_semaphore()

    def greet(k, carry):
        pl.semaphore_signal(barrier, inc=1, device_id=(b, peer(k)), device_id_type=MESH)
        return carry

    lax.fori_loop(0, n_narrow - 1, greet, 0)
    for other in (above, below):
        pl.semaphore_signal(barrier, inc=1, device_id=(other, n), device_id_type=MESH)

    picture = pic_ref[...].astype(F32)
    image_norm = jnp.sqrt(jnp.sum(picture * picture, axis=1, keepdims=True) + EPS)
    image_low[0] = (picture / image_norm).astype(BF16)

    spot = lambda axis: lax.broadcasted_iota(jnp.int32, (cols, cols), axis)
    turn = (spot(0) == spot(1)).astype(F32).astype(BF16)

    def pack(k, carry):
        block = cap_ref[pl.ds(pl.multiple_of(k * rows, rows), rows), :]
        packed[k] = fold(dot(turn, block, (1, 1))).astype(BF16)
        return carry

    lax.fori_loop(0, n_narrow, pack, 0)
    got[n] = packed[n]

    pl.semaphore_wait(barrier, n_narrow + 1)

    def block_copy(source, target, sent, received, p, here):
        return pltpu.make_async_remote_copy(
            src_ref=source.at[p], dst_ref=target.at[here], send_sem=sent.at[p], recv_sem=received.at[here],
            device_id=(b, p), device_id_type=MESH)

    def whole_copy(buffer, sent, received, slot, other):
        return pltpu.make_async_remote_copy(
            src_ref=buffer.at[0], dst_ref=buffer.at[slot], send_sem=sent.at[slot - 1], recv_sem=received.at[slot - 1],
            device_id=(other, n), device_id_type=MESH)

    def send_packed(k, carry):
        p = peer(k)
        block_copy(packed, got, pack_sent, pack_got, p, n).start()
        return carry

    lax.fori_loop(0, n_narrow // 2, send_packed, 0)
    image_up = whole_copy(image_low, image_sent, image_got, 1, above)
    image_down = whole_copy(image_low, image_sent, image_got, 2, below)
    image_up.start()
    image_down.start()
    lax.fori_loop(n_narrow // 2, n_narrow - 1, send_packed, 0)

    image_turned[:, :rows] = image_low[0].T

    for slot, copy in ((1, image_up), (2, image_down)):
        copy.wait_recv()
        image_turned[:, slot * rows:(slot + 1) * rows] = image_low[slot].T

    def take_packed(k, carry):
        p = peer(k)

        @pl.when(k < n_narrow - 1)
        def _():
            block_copy(packed, got, pack_sent, pack_got, p, p).wait_recv()

        raw[pl.ds(pl.multiple_of(p * cols, 8), cols), :] = unfold(got[p].astype(F32))
        return carry

    lax.fori_loop(0, n_narrow, take_packed, 0)

    text = raw[...]
    text_norm = jnp.sqrt(jnp.sum(text * text, axis=0, keepdims=True) + EPS)
    text_low[0] = (text / text_norm).astype(BF16)
    text_up = whole_copy(text_low, text_sent, text_got, 1, above)
    text_down = whole_copy(text_low, text_sent, text_got, 2, below)
    text_up.start()
    text_down.start()

    sharp, offset = sharp_ref[0], offset_ref[0]
    place = lambda axis: lax.broadcasted_iota(jnp.int32, (rows, rows), axis)
    same = (place(0) == place(1)).astype(F32)

    def tile(image, words):
        return sharp * dot(image, words, (1, 0)) + offset

    def coefs(logits):
        return (sharp * jax.nn.sigmoid(logits)).astype(BF16)

    own_logits = tile(image_low[0], text_low[0])
    own_coef = (sharp * (jax.nn.sigmoid(own_logits) - same)).astype(BF16)
    all_coef = jnp.concatenate(
        [own_coef] + [coefs(tile(image_low[s], text_low[0])) for s in (1, 2)], axis=0)
    text_sum = dot(image_turned[...], all_coef, (1, 0))
    unit = raw[...] / text_norm
    inner = jnp.sum(unit * text_sum, axis=0, keepdims=True)
    text_back = (text_sum - unit * inner) / text_norm
    for p in range(n_narrow):
        back_out[p] = fold(text_back[p * cols:(p + 1) * cols]).astype(BF16)
    back_in[n] = back_out[n]

    def send_back(k, carry):
        block_copy(back_out, back_in, back_sent, back_got, peer(k), n).start()
        return carry

    lax.fori_loop(0, n_narrow - 1, send_back, 0)

    losses = softplus((1.0 - 2.0 * same) * own_logits)
    image_sum = dot(own_coef, text_low[0], (1, 1))
    for slot, copy in ((1, text_up), (2, text_down)):
        copy.wait_recv()
        logits = tile(image_low[0], text_low[slot])
        losses = losses + softplus(logits)
        image_sum = image_sum + dot(coefs(logits), text_low[slot], (1, 1))
    loss_ref[...] = jnp.sum(losses.T, axis=0, keepdims=True)
    picture = pic_ref[...].astype(F32)
    image_unit = picture / image_norm
    image_inner = jnp.sum(image_unit * image_sum, axis=1, keepdims=True)
    image_grad_ref[...] = (image_sum - image_unit * image_inner) / image_norm

    half = rows // 2

    def take_back(k, carry):
        p = peer(k)

        @pl.when(k < n_narrow - 1)
        def _():
            block_copy(back_out, back_in, back_sent, back_got, p, p).wait_recv()

        block = back_in[p].astype(F32)
        for part in range(2):
            text_grad_ref[pl.ds(pl.multiple_of(p * rows + part * half, half), half), :] = (
                block[part * cols:(part + 1) * cols].T)
        return carry

    lax.fori_loop(0, n_narrow, take_back, 0)

    def sent_all(k, carry):
        p = peer(k)
        block_copy(packed, got, pack_sent, pack_got, p, n).wait_send()
        block_copy(back_out, back_in, back_sent, back_got, p, n).wait_send()
        return carry

    lax.fori_loop(0, n_narrow - 1, sent_all, 0)
    for copy in (image_up, image_down, text_up, text_down):
        copy.wait_send()


def solution(mesh):
    n_blk, n_narrow = mesh.shape["blk"], mesh.shape["narrow"]

    def step(pictures, captions, sharpness, offset):
        rows, depth = pictures.shape
        cols = captions.shape[1]
        vmem, smem = pl.BlockSpec(memory_space=pltpu.VMEM), pl.BlockSpec(memory_space=pltpu.SMEM)
        blocks = pltpu.VMEM((n_narrow, 2 * cols, rows // 2), BF16)
        loss, image_grad, text_grad = pl.pallas_call(
            functools.partial(kernel, n_blk, n_narrow),
            out_shape=(
                jax.ShapeDtypeStruct((1, rows), F32),
                jax.ShapeDtypeStruct((rows, depth), F32),
                jax.ShapeDtypeStruct(captions.shape, F32),
            ),
            in_specs=[vmem, vmem, smem, smem],
            out_specs=(vmem, vmem, vmem),
            scratch_shapes=[
                pltpu.VMEM((3, rows, depth), BF16),
                pltpu.VMEM((depth, 3 * rows), BF16),
                blocks,
                blocks,
                pltpu.VMEM((depth, rows), F32),
                pltpu.VMEM((3, depth, rows), BF16),
                blocks,
                blocks,
                pltpu.SemaphoreType.DMA((n_narrow,)),
                pltpu.SemaphoreType.DMA((n_narrow,)),
                pltpu.SemaphoreType.DMA((2,)),
                pltpu.SemaphoreType.DMA((2,)),
                pltpu.SemaphoreType.DMA((2,)),
                pltpu.SemaphoreType.DMA((2,)),
                pltpu.SemaphoreType.DMA((n_narrow,)),
                pltpu.SemaphoreType.DMA((n_narrow,)),
            ],
            compiler_params=pltpu.CompilerParams(
                collective_id=0, has_side_effects=True, vmem_limit_bytes=48 * 2**20),
        )(pictures, captions, sharpness, offset)
        return loss.reshape(rows), image_grad, text_grad

    return jax.shard_map(
        step,
        mesh=mesh,
        in_specs=(P(("blk", "narrow"), None), P("blk", "narrow"), P(), P()),
        out_specs=(P(("blk", "narrow")), P(("blk", "narrow"), None), P("blk", "narrow")),
        check_vma=False,
    )
```

```python
import functools

import jax
import jax.numpy as jnp
from jax import lax
from jax.experimental import pallas as pl
from jax.experimental.pallas import tpu as pltpu
from jax.sharding import PartitionSpec as P

EPS = 1e-06
MESH = pl.DeviceIdType.MESH
F32, BF16 = jnp.float32, jnp.bfloat16


def fold(chunk):
    half = chunk.shape[1] // 2
    return jnp.concatenate([chunk[:, :half], chunk[:, half:]], axis=0)


def unfold(chunk):
    cols = chunk.shape[0] // 2
    return jnp.concatenate([chunk[:cols], chunk[cols:]], axis=1)


def dot(left, right, contract):
    return lax.dot_general(left, right, ((contract[:1], contract[1:]), ((), ())), preferred_element_type=F32)


def softplus(x):
    return jnp.maximum(x, 0.0) + jnp.log1p(jnp.exp(-jnp.abs(x)))


def kernel(
    n_blk, n_narrow,
    pic_ref, cap_ref, sharp_ref, offset_ref,
    loss_ref, image_grad_ref, text_grad_ref,
    image_low, image_turned, packed, got, raw, text_low, back_out, back_in,
    pack_sent, pack_got, image_sent, image_got, text_sent, text_got, back_sent, back_got,
):
    b, n = lax.axis_index("blk"), lax.axis_index("narrow")
    rows, depth = pic_ref.shape
    cols = depth // n_narrow
    above, below = lax.rem(b + 1, n_blk), lax.rem(b + n_blk - 1, n_blk)
    far = 1 - lax.rem(n, 2)

    def peer(k):
        side = jnp.where(k < n_narrow // 2, far, 1 - far)
        step = lax.rem(k + 1, n_narrow // 2)
        return lax.rem(n // 2 + step, n_narrow // 2) * 2 + side

    barrier = pltpu.get_barrier_semaphore()

    def greet(k, carry):
        pl.semaphore_signal(barrier, inc=1, device_id=(b, peer(k)), device_id_type=MESH)
        return carry

    lax.fori_loop(0, n_narrow - 1, greet, 0)
    for other in (above, below):
        pl.semaphore_signal(barrier, inc=1, device_id=(other, n), device_id_type=MESH)

    picture = pic_ref[...].astype(F32)
    image_norm = jnp.sqrt(jnp.sum(picture * picture, axis=1, keepdims=True) + EPS)
    image_low[0] = (picture / image_norm).astype(BF16)

    def pack(k, carry):
        block = cap_ref[:, pl.ds(pl.multiple_of(k * rows, rows), rows)]
        packed[k] = fold(block.astype(F32)).astype(BF16)
        return carry

    lax.fori_loop(0, n_narrow, pack, 0)
    got[n] = packed[n]

    pl.semaphore_wait(barrier, n_narrow + 1)

    def block_copy(source, target, sent, received, p, here):
        return pltpu.make_async_remote_copy(
            src_ref=source.at[p], dst_ref=target.at[here], send_sem=sent.at[p], recv_sem=received.at[here],
            device_id=(b, p), device_id_type=MESH)

    def whole_copy(buffer, sent, received, slot, other):
        return pltpu.make_async_remote_copy(
            src_ref=buffer.at[0], dst_ref=buffer.at[slot], send_sem=sent.at[slot - 1], recv_sem=received.at[slot - 1],
            device_id=(other, n), device_id_type=MESH)

    def send_packed(k, carry):
        p = peer(k)
        block_copy(packed, got, pack_sent, pack_got, p, n).start()
        return carry

    lax.fori_loop(0, n_narrow // 2, send_packed, 0)
    image_up = whole_copy(image_low, image_sent, image_got, 1, above)
    image_down = whole_copy(image_low, image_sent, image_got, 2, below)
    image_up.start()
    image_down.start()
    lax.fori_loop(n_narrow // 2, n_narrow - 1, send_packed, 0)

    image_turned[:, :rows] = image_low[0].T

    for slot, copy in ((1, image_up), (2, image_down)):
        copy.wait_recv()
        image_turned[:, slot * rows:(slot + 1) * rows] = image_low[slot].T

    def take_packed(k, carry):
        p = peer(k)

        @pl.when(k < n_narrow - 1)
        def _():
            block_copy(packed, got, pack_sent, pack_got, p, p).wait_recv()

        raw[pl.ds(pl.multiple_of(p * cols, 8), cols), :] = unfold(got[p].astype(F32))
        return carry

    lax.fori_loop(0, n_narrow, take_packed, 0)

    text = raw[...]
    text_norm = jnp.sqrt(jnp.sum(text * text, axis=0, keepdims=True) + EPS)
    text_low[0] = (text / text_norm).astype(BF16)
    text_up = whole_copy(text_low, text_sent, text_got, 1, above)
    text_down = whole_copy(text_low, text_sent, text_got, 2, below)
    text_up.start()
    text_down.start()

    sharp, offset = sharp_ref[0], offset_ref[0]
    place = lambda axis: lax.broadcasted_iota(jnp.int32, (rows, rows), axis)
    same = (place(0) == place(1)).astype(F32)

    def tile(image, words):
        return sharp * dot(image, words, (1, 0)) + offset

    def coefs(logits):
        return (sharp * jax.nn.sigmoid(logits)).astype(BF16)

    own_logits = tile(image_low[0], text_low[0])
    own_coef = (sharp * (jax.nn.sigmoid(own_logits) - same)).astype(BF16)
    all_coef = jnp.concatenate(
        [own_coef] + [coefs(tile(image_low[s], text_low[0])) for s in (1, 2)], axis=0)
    text_sum = dot(image_turned[...], all_coef, (1, 0))
    unit = raw[...] / text_norm
    inner = jnp.sum(unit * text_sum, axis=0, keepdims=True)
    text_back = (text_sum - unit * inner) / text_norm
    for p in range(n_narrow):
        back_out[p] = fold(text_back[p * cols:(p + 1) * cols]).astype(BF16)
    back_in[n] = back_out[n]

    def send_back(k, carry):
        block_copy(back_out, back_in, back_sent, back_got, peer(k), n).start()
        return carry

    lax.fori_loop(0, n_narrow - 1, send_back, 0)

    losses = softplus((1.0 - 2.0 * same) * own_logits)
    image_sum = dot(own_coef, text_low[0], (1, 1))
    for slot, copy in ((1, text_up), (2, text_down)):
        copy.wait_recv()
        logits = tile(image_low[0], text_low[slot])
        losses = losses + softplus(logits)
        image_sum = image_sum + dot(coefs(logits), text_low[slot], (1, 1))
    loss_ref[...] = jnp.sum(losses.T, axis=0, keepdims=True)
    picture = pic_ref[...].astype(F32)
    image_unit = picture / image_norm
    image_inner = jnp.sum(image_unit * image_sum, axis=1, keepdims=True)
    image_grad_ref[...] = (image_sum - image_unit * image_inner) / image_norm

    def take_back(k, carry):
        p = peer(k)

        @pl.when(k < n_narrow - 1)
        def _():
            block_copy(back_out, back_in, back_sent, back_got, p, p).wait_recv()

        text_grad_ref[:, pl.ds(pl.multiple_of(p * rows, rows), rows)] = unfold(back_in[p].astype(F32))
        return carry

    lax.fori_loop(0, n_narrow, take_back, 0)

    def sent_all(k, carry):
        p = peer(k)
        block_copy(packed, got, pack_sent, pack_got, p, n).wait_send()
        block_copy(back_out, back_in, back_sent, back_got, p, n).wait_send()
        return carry

    lax.fori_loop(0, n_narrow - 1, sent_all, 0)
    for copy in (image_up, image_down, text_up, text_down):
        copy.wait_send()


def solution(mesh):
    n_blk, n_narrow = mesh.shape["blk"], mesh.shape["narrow"]

    def step(pictures, captions, sharpness, offset):
        rows, depth = pictures.shape
        cols = captions.shape[1]
        vmem, smem = pl.BlockSpec(memory_space=pltpu.VMEM), pl.BlockSpec(memory_space=pltpu.SMEM)
        blocks = pltpu.VMEM((n_narrow, 2 * cols, rows // 2), BF16)
        loss, image_grad, text_grad = pl.pallas_call(
            functools.partial(kernel, n_blk, n_narrow),
            out_shape=(
                jax.ShapeDtypeStruct((1, rows), F32),
                jax.ShapeDtypeStruct((rows, depth), F32),
                jax.ShapeDtypeStruct(captions.shape[::-1], F32),
            ),
            in_specs=[vmem, vmem, smem, smem],
            out_specs=(vmem, vmem, vmem),
            scratch_shapes=[
                pltpu.VMEM((3, rows, depth), BF16),
                pltpu.VMEM((depth, 3 * rows), BF16),
                blocks,
                blocks,
                pltpu.VMEM((depth, rows), F32),
                pltpu.VMEM((3, depth, rows), BF16),
                blocks,
                blocks,
                pltpu.SemaphoreType.DMA((n_narrow,)),
                pltpu.SemaphoreType.DMA((n_narrow,)),
                pltpu.SemaphoreType.DMA((2,)),
                pltpu.SemaphoreType.DMA((2,)),
                pltpu.SemaphoreType.DMA((2,)),
                pltpu.SemaphoreType.DMA((2,)),
                pltpu.SemaphoreType.DMA((n_narrow,)),
                pltpu.SemaphoreType.DMA((n_narrow,)),
            ],
            compiler_params=pltpu.CompilerParams(
                collective_id=0, has_side_effects=True, vmem_limit_bytes=48 * 2**20),
        )(pictures, captions.T, sharpness, offset)
        return loss.reshape(rows), image_grad, text_grad.T

    return jax.shard_map(
        step,
        mesh=mesh,
        in_specs=(P(("blk", "narrow"), None), P("blk", "narrow"), P(), P()),
        out_specs=(P(("blk", "narrow")), P(("blk", "narrow"), None), P("blk", "narrow")),
        check_vma=False,
    )
```

```python
import functools

import jax
import jax.numpy as jnp
from jax import lax
from jax.experimental import pallas as pl
from jax.experimental.pallas import tpu as pltpu
from jax.sharding import PartitionSpec as P

EPS = 1e-06
RUN = 12
MESH = pl.DeviceIdType.MESH
F32, BF16 = jnp.float32, jnp.bfloat16


def fold(chunk):
    half = chunk.shape[1] // 2
    return jnp.concatenate([chunk[:, :half], chunk[:, half:]], axis=0)


def unfold(chunk):
    cols = chunk.shape[0] // 2
    return jnp.concatenate([chunk[:cols], chunk[cols:]], axis=1)


def dot(left, right, contract):
    return lax.dot_general(left, right, ((contract[:1], contract[1:]), ((), ())), preferred_element_type=F32)


def softplus(x):
    return jnp.maximum(x, 0.0) + jnp.log1p(jnp.exp(-jnp.abs(x)))


def kernel(
    n_blk, n_narrow, run,
    pic_hbm, cap_hbm, sharp_ref, offset_ref,
    loss_ref, image_grad_ref, text_grad_ref,
    pic_ref, cap_ref, image_low, image_turned, packed, got, raw, text_low, back_out, back_in,
    edge_got, edge_raw, edge_out, edge_in,
    load_sem, pack_sent, pack_got, image_sent, image_got, text_sent, text_got, back_sent, back_got,
    edge_sent, edge_came, edge_back_sent, edge_back_got,
):
    load_picture = pltpu.make_async_copy(pic_hbm, pic_ref, load_sem.at[0])
    load_captions = pltpu.make_async_copy(cap_hbm, cap_ref, load_sem.at[1])
    load_captions.start()
    load_picture.start()

    b, n = lax.axis_index("blk"), lax.axis_index("narrow")
    rows, depth = pic_ref.shape
    cols = depth // n_narrow
    above, below = lax.rem(b + 1, n_blk), lax.rem(b + n_blk - 1, n_blk)
    top, bottom = lax.rem(b, run) == run - 1, lax.rem(b, run) == 0
    edge = jnp.logical_or(top, bottom)
    across = jnp.where(top, above, below)
    across_slot = jnp.where(top, 2, 1)
    far = 1 - lax.rem(n, 2)

    def peer(k):
        side = jnp.where(k < n_narrow // 2, far, 1 - far)
        step = lax.rem(k + 1, n_narrow // 2)
        return lax.rem(n // 2 + step, n_narrow // 2) * 2 + side

    def each(count, body, first=0):
        def step(k, carry):
            body(k)
            return carry
        lax.fori_loop(first, count, step, 0)

    barrier = pltpu.get_barrier_semaphore()

    def greet(blk, narrow):
        pl.semaphore_signal(barrier, inc=1, device_id=(blk, narrow), device_id_type=MESH)

    each(n_narrow - 1, lambda k: greet(b, peer(k)))

    @pl.when(jnp.logical_not(top))
    def _():
        greet(above, n)

    @pl.when(jnp.logical_not(bottom))
    def _():
        greet(below, n)

    @pl.when(edge)
    def _():
        each(n_narrow, lambda k: greet(across, peer(k)))

    load_captions.wait()

    def pack(k):
        block = cap_ref[:, pl.ds(pl.multiple_of(k * rows, rows), rows)]
        packed[k] = fold(block.astype(F32)).astype(BF16)

    each(n_narrow, pack)
    got[n] = packed[n]

    load_picture.wait()
    picture = pic_ref[...].astype(F32)
    image_norm = jnp.sqrt(jnp.sum(picture * picture, axis=1, keepdims=True) + EPS)
    image_low[0] = (picture / image_norm).astype(BF16)

    @pl.when(edge)
    def _():
        image_low[across_slot] = jnp.zeros((rows, depth), BF16)

    @pl.when(edge)
    def _():
        pl.semaphore_wait(barrier, 2 * n_narrow)

    @pl.when(jnp.logical_not(edge))
    def _():
        pl.semaphore_wait(barrier, n_narrow + 1)

    def block_copy(source, target, sent, received, blk, p, here):
        return pltpu.make_async_remote_copy(
            src_ref=source.at[p], dst_ref=target.at[here], send_sem=sent.at[p], recv_sem=received.at[here],
            device_id=(blk, p), device_id_type=MESH)

    def pack_copy(p, here):
        return block_copy(packed, got, pack_sent, pack_got, b, p, here)

    def edge_copy(p, here):
        return block_copy(packed, edge_got, edge_sent, edge_came, across, p, here)

    def back_copy(p, here):
        return block_copy(back_out, back_in, back_sent, back_got, b, p, here)

    def edge_back_copy(p, here):
        return block_copy(edge_out, edge_in, edge_back_sent, edge_back_got, across, p, here)

    def whole_copy(buffer, sent, received, slot):
        return pltpu.make_async_remote_copy(
            src_ref=buffer.at[0], dst_ref=buffer.at[slot], send_sem=sent.at[slot - 1], recv_sem=received.at[slot - 1],
            device_id=(above if slot == 1 else below, n), device_id_type=MESH)

    def to_neighbours(act):
        @pl.when(jnp.logical_not(top))
        def _():
            act(1)

        @pl.when(jnp.logical_not(bottom))
        def _():
            act(2)

    def from_neighbours(slot, act):
        pl.when(jnp.logical_not(bottom if slot == 1 else top))(act)

    each(n_narrow // 2, lambda k: pack_copy(peer(k), n).start())
    each(n_narrow - 1, lambda k: pack_copy(peer(k), n).start(), n_narrow // 2)
    to_neighbours(lambda slot: whole_copy(image_low, image_sent, image_got, slot).start())

    @pl.when(edge)
    def _():
        each(n_narrow, lambda k: edge_copy(peer(k), n).start())


    image_turned[:, :rows] = image_low[0].T
    for slot in (1, 2):
        from_neighbours(slot, lambda: whole_copy(image_low, image_sent, image_got, slot).wait_recv())
        image_turned[:, slot * rows:(slot + 1) * rows] = image_low[slot].T

    def unpack(source, target, p):
        target[pl.ds(pl.multiple_of(p * cols, 8), cols), :] = unfold(source[p].astype(F32))

    def take_packed(k):
        p = peer(k)
        pack_copy(p, p).wait_recv()
        unpack(got, raw, p)

    unpack(got, raw, n)
    each(n_narrow - 1, take_packed)

    def unit_words(words):
        norm = jnp.sqrt(jnp.sum(words * words, axis=0, keepdims=True) + EPS)
        return words / norm, norm

    def split_out(target, text_sum, words):
        unit, norm = unit_words(words)
        inner = jnp.sum(unit * text_sum, axis=0, keepdims=True)
        grad = (text_sum - unit * inner) / norm
        for p in range(n_narrow):
            target[p] = fold(grad[p * cols:(p + 1) * cols]).astype(BF16)

    text_low[0] = unit_words(raw[...])[0].astype(BF16)
    to_neighbours(lambda slot: whole_copy(text_low, text_sent, text_got, slot).start())

    sharp, offset = sharp_ref[0], offset_ref[0]
    place = lambda axis: lax.broadcasted_iota(jnp.int32, (rows, rows), axis)
    same = (place(0) == place(1)).astype(F32)

    def tile(image, words):
        return sharp * dot(image, words, (1, 0)) + offset

    def coefs(logits):
        return (sharp * jax.nn.sigmoid(logits)).astype(BF16)

    own_logits = tile(image_low[0], text_low[0])
    own_coef = (sharp * (jax.nn.sigmoid(own_logits) - same)).astype(BF16)
    all_coef = jnp.concatenate(
        [own_coef] + [coefs(tile(image_low[s], text_low[0])) for s in (1, 2)], axis=0)
    split_out(back_out, dot(image_turned[...], all_coef, (1, 0)), raw[...])
    back_in[n] = back_out[n]
    each(n_narrow - 1, lambda k: back_copy(peer(k), n).start())

    @pl.when(edge)
    def _():
        def take_across(k):
            p = peer(k)
            edge_copy(p, p).wait_recv()
            unpack(edge_got, edge_raw, p)

        each(n_narrow, take_across)
        words = unit_words(edge_raw[...])[0].astype(BF16)
        text_low[across_slot] = words
        part = dot(image_turned[:, :rows], coefs(tile(image_low[0], words)), (1, 0))
        split_out(edge_out, part, edge_raw[...])
        each(n_narrow, lambda k: edge_back_copy(peer(k), n).start())

    losses = softplus((1.0 - 2.0 * same) * own_logits)
    image_sum = dot(own_coef, text_low[0], (1, 1))
    for slot in (1, 2):
        from_neighbours(slot, lambda: whole_copy(text_low, text_sent, text_got, slot).wait_recv())
        logits = tile(image_low[0], text_low[slot])
        losses = losses + softplus(logits)
        image_sum = image_sum + dot(coefs(logits), text_low[slot], (1, 1))
    loss_ref[...] = jnp.sum(losses.T, axis=0, keepdims=True)
    image_unit = pic_ref[...].astype(F32) / image_norm
    image_inner = jnp.sum(image_unit * image_sum, axis=1, keepdims=True)
    image_grad_ref[...] = (image_sum - image_unit * image_inner) / image_norm

    def block_of(p):
        return (slice(None), pl.ds(pl.multiple_of(p * rows, rows), rows))

    def take_back(k):
        p = peer(k)
        back_copy(p, p).wait_recv()
        text_grad_ref[block_of(p)] = unfold(back_in[p].astype(F32))

    text_grad_ref[block_of(n)] = unfold(back_in[n].astype(F32))
    each(n_narrow - 1, take_back)

    @pl.when(edge)
    def _():
        def take_edge(k):
            p = peer(k)
            edge_back_copy(p, p).wait_recv()
            text_grad_ref[block_of(p)] += unfold(edge_in[p].astype(F32))

        each(n_narrow, take_edge)

    def sent_all(k):
        pack_copy(peer(k), n).wait_send()
        back_copy(peer(k), n).wait_send()

    each(n_narrow - 1, sent_all)

    def sent_whole(slot):
        whole_copy(image_low, image_sent, image_got, slot).wait_send()
        whole_copy(text_low, text_sent, text_got, slot).wait_send()

    to_neighbours(sent_whole)

    @pl.when(edge)
    def _():
        def sent_across(k):
            edge_copy(peer(k), n).wait_send()
            edge_back_copy(peer(k), n).wait_send()

        each(n_narrow, sent_across)


def hand_out(loss, image_grad, text_grad, loss_out, image_out, text_out, sems):
    copies = [
        pltpu.make_async_copy(source, target, sems.at[i])
        for i, (source, target) in enumerate(((text_grad, text_out), (image_grad, image_out), (loss, loss_out)))]
    for copy in copies:
        copy.start()
    for copy in copies:
        copy.wait()


def solution(mesh):
    n_blk, n_narrow = mesh.shape["blk"], mesh.shape["narrow"]

    def step(pictures, captions, sharpness, offset):
        rows, depth = pictures.shape
        words = captions.T
        vmem, smem = pl.BlockSpec(memory_space=pltpu.VMEM), pl.BlockSpec(memory_space=pltpu.SMEM)
        hbm = pl.BlockSpec(memory_space=pltpu.HBM)
        blocks = pltpu.VMEM((n_narrow, 2 * words.shape[0], rows // 2), BF16)
        per_peer, per_side = pltpu.SemaphoreType.DMA((n_narrow,)), pltpu.SemaphoreType.DMA((2,))
        outs = (
            jax.ShapeDtypeStruct((1, rows), F32),
            jax.ShapeDtypeStruct((rows, depth), F32),
            jax.ShapeDtypeStruct(words.shape, F32),
        )
        results = pl.pallas_call(
            functools.partial(kernel, n_blk, n_narrow, RUN),
            out_shape=outs,
            in_specs=[hbm, hbm, smem, smem],
            out_specs=(vmem, vmem, vmem),
            scratch_shapes=[
                pltpu.VMEM(pictures.shape, BF16),
                pltpu.VMEM(words.shape, BF16),
                pltpu.VMEM((3, rows, depth), BF16),
                pltpu.VMEM((depth, 3 * rows), BF16),
                blocks,
                blocks,
                pltpu.VMEM((depth, rows), F32),
                pltpu.VMEM((3, depth, rows), BF16),
                blocks,
                blocks,
                blocks,
                pltpu.VMEM((depth, rows), F32),
                blocks,
                blocks,
                per_side,
                per_peer, per_peer,
                per_side, per_side,
                per_side, per_side,
                per_peer, per_peer,
                per_peer, per_peer,
                per_peer, per_peer,
            ],
            compiler_params=pltpu.CompilerParams(
                collective_id=0, has_side_effects=True, vmem_limit_bytes=48 * 2**20),
        )(*(pltpu.with_memory_space_constraint(x, pltpu.HBM) for x in (pictures, words)), sharpness, offset)
        loss, image_grad, text_grad = pl.pallas_call(
            hand_out,
            out_shape=outs,
            in_specs=[vmem] * 3,
            out_specs=(hbm,) * 3,
            scratch_shapes=[pltpu.SemaphoreType.DMA((3,))],
            compiler_params=pltpu.CompilerParams(vmem_limit_bytes=2**20),
        )(*results)
        return loss.reshape(rows), image_grad, text_grad.T

    return jax.shard_map(
        step,
        mesh=mesh,
        in_specs=(P(("blk", "narrow"), None), P("blk", "narrow"), P(), P()),
        out_specs=(P(("blk", "narrow")), P(("blk", "narrow"), None), P("blk", "narrow")),
        check_vma=False,
    )
```

```python
import functools

import jax
import jax.numpy as jnp
from jax import lax
from jax.experimental import pallas as pl
from jax.experimental.pallas import tpu as pltpu
from jax.sharding import PartitionSpec as P

EPS = 1e-06
RUN = 12
MESH = pl.DeviceIdType.MESH
F32, BF16 = jnp.float32, jnp.bfloat16


def fold(chunk):
    half = chunk.shape[1] // 2
    return jnp.concatenate([chunk[:, :half], chunk[:, half:]], axis=0)


def unfold(chunk):
    cols = chunk.shape[0] // 2
    return jnp.concatenate([chunk[:cols], chunk[cols:]], axis=1)


def dot(left, right, contract):
    return lax.dot_general(left, right, ((contract[:1], contract[1:]), ((), ())), preferred_element_type=F32)


def softplus(x):
    return jnp.maximum(x, 0.0) + jnp.log1p(jnp.exp(-jnp.abs(x)))


def kernel(
    n_blk, n_narrow, run,
    pic_hbm, cap_hbm, sharp_ref, offset_ref,
    loss_ref, image_grad_ref, text_grad_ref,
    pic_ref, cap_ref, image_low, image_turned, packed, got, raw, text_low, back_out, back_in,
    edge_got, edge_raw, edge_out, edge_in,
    load_sem, pack_sent, pack_got, image_sent, image_got, text_sent, text_got, back_sent, back_got,
    edge_sent, edge_came, edge_back_sent, edge_back_got, beside,
):
    load_picture = pltpu.make_async_copy(pic_hbm, pic_ref, load_sem.at[0])
    load_captions = pltpu.make_async_copy(cap_hbm, cap_ref, load_sem.at[1])
    load_captions.start()
    load_picture.start()

    b, n = lax.axis_index("blk"), lax.axis_index("narrow")
    rows, depth = pic_ref.shape
    cols = depth // n_narrow
    above, below = lax.rem(b + 1, n_blk), lax.rem(b + n_blk - 1, n_blk)
    top, bottom = lax.rem(b, run) == run - 1, lax.rem(b, run) == 0
    edge = jnp.logical_or(top, bottom)
    across = jnp.where(top, above, below)
    across_slot = jnp.where(top, 2, 1)
    far = 1 - lax.rem(n, 2)

    def peer(k):
        side = jnp.where(k < n_narrow // 2, far, 1 - far)
        step = lax.rem(k + 1, n_narrow // 2)
        return lax.rem(n // 2 + step, n_narrow // 2) * 2 + side

    half = n_narrow // 2
    own_side = lax.rem(n, 2) * half

    def spot(p):
        return lax.rem(p, 2) * half + p // 2

    def each(count, body, first=0):
        def step(k, carry):
            body(k)
            return carry
        lax.fori_loop(first, count, step, 0)

    barrier = pltpu.get_barrier_semaphore()

    def greet(blk, narrow):
        pl.semaphore_signal(barrier, inc=1, device_id=(blk, narrow), device_id_type=MESH)

    each(n_narrow - 1, lambda k: greet(b, peer(k)))

    @pl.when(jnp.logical_not(top))
    def _():
        greet(above, n)

    @pl.when(jnp.logical_not(bottom))
    def _():
        greet(below, n)

    @pl.when(edge)
    def _():
        each(n_narrow, lambda k: greet(across, peer(k)))

    load_captions.wait()

    def pack(k):
        block = cap_ref[:, pl.ds(pl.multiple_of(k * rows, rows), rows)]
        packed[k] = fold(block.astype(F32)).astype(BF16)

    each(n_narrow, pack)
    got[spot(n)] = packed[n]

    @pl.when(edge)
    def _():
        pl.semaphore_wait(barrier, 2 * n_narrow)

    @pl.when(jnp.logical_not(edge))
    def _():
        pl.semaphore_wait(barrier, n_narrow + 1)

    def block_copy(source, target, sent, received, blk, p, here):
        return pltpu.make_async_remote_copy(
            src_ref=source.at[p], dst_ref=target.at[here], send_sem=sent.at[p], recv_sem=received.at[here],
            device_id=(blk, p), device_id_type=MESH)

    def pack_copy(p, here):
        return pltpu.make_async_remote_copy(
            src_ref=packed.at[p], dst_ref=got.at[spot(here)], send_sem=pack_sent.at[p], recv_sem=pack_got.at[here],
            device_id=(b, p), device_id_type=MESH)

    def edge_copy(p, here):
        return block_copy(packed, edge_got, edge_sent, edge_came, across, p, here)

    def back_copy(p, here):
        return block_copy(back_out, back_in, back_sent, back_got, b, p, here)

    def edge_back_copy(p, here):
        return block_copy(edge_out, edge_in, edge_back_sent, edge_back_got, across, p, here)

    def whole_copy(buffer, sent, received, slot):
        return pltpu.make_async_remote_copy(
            src_ref=buffer.at[0], dst_ref=buffer.at[slot], send_sem=sent.at[slot - 1], recv_sem=received.at[slot - 1],
            device_id=(above if slot == 1 else below, n), device_id_type=MESH)

    def text_copy(slot, far_side):
        part = pl.ds(half - own_side if far_side else own_side, half)
        sem = 2 * (slot - 1) + far_side
        return pltpu.make_async_remote_copy(
            src_ref=got.at[part], dst_ref=beside.at[slot - 1, part], send_sem=text_sent.at[sem], recv_sem=text_got.at[sem],
            device_id=(above if slot == 1 else below, n), device_id_type=MESH)

    def to_neighbours(act):
        @pl.when(jnp.logical_not(top))
        def _():
            act(1)

        @pl.when(jnp.logical_not(bottom))
        def _():
            act(2)

    def from_neighbours(slot, act):
        pl.when(jnp.logical_not(bottom if slot == 1 else top))(act)

    each(n_narrow // 2, lambda k: pack_copy(peer(k), n).start())
    each(n_narrow - 1, lambda k: pack_copy(peer(k), n).start(), n_narrow // 2)

    load_picture.wait()
    picture = pic_ref[...].astype(F32)
    image_norm = jnp.sqrt(jnp.sum(picture * picture, axis=1, keepdims=True) + EPS)
    image_scale = 1.0 / image_norm
    image_low[0] = (picture * image_scale).astype(BF16)

    @pl.when(edge)
    def _():
        image_low[across_slot] = jnp.zeros((rows, depth), BF16)

    to_neighbours(lambda slot: whole_copy(image_low, image_sent, image_got, slot).start())

    @pl.when(edge)
    def _():
        each(n_narrow, lambda k: edge_copy(peer(k), n).start())


    def unpack(source, target, p, place):
        target[pl.ds(pl.multiple_of(p * cols, 8), cols), :] = unfold(source[place].astype(F32))

    def take_packed(k):
        p = peer(k)
        pack_copy(p, p).wait_recv()
        unpack(got, raw, p, spot(p))

    image_turned[:, :rows] = image_low[0].T
    unpack(got, raw, n, spot(n))
    each(n_narrow - 1, take_packed, half)
    to_neighbours(lambda slot: text_copy(slot, 0).start())

    for slot in (1, 2):
        from_neighbours(slot, lambda: whole_copy(image_low, image_sent, image_got, slot).wait_recv())
        image_turned[:, slot * rows:(slot + 1) * rows] = image_low[slot].T

    each(half, take_packed)
    to_neighbours(lambda slot: text_copy(slot, 1).start())

    def unit_words(words):
        scale = 1.0 / jnp.sqrt(jnp.sum(words * words, axis=0, keepdims=True) + EPS)
        return words * scale, scale

    def split_out(target, text_sum, words):
        unit, scale = unit_words(words)
        inner = jnp.sum(unit * text_sum, axis=0, keepdims=True)
        grad = (text_sum - unit * inner) * scale
        for p in range(n_narrow):
            target[p] = fold(grad[p * cols:(p + 1) * cols]).astype(BF16)

    text_low[0] = unit_words(raw[...])[0].astype(BF16)

    sharp, offset = sharp_ref[0], offset_ref[0]
    place = lambda axis: lax.broadcasted_iota(jnp.int32, (rows, rows), axis)
    same = (place(0) == place(1)).astype(F32)

    def tile(image, words):
        return sharp * dot(image, words, (1, 0)) + offset

    def coefs(logits):
        return (sharp * jax.nn.sigmoid(logits)).astype(BF16)

    logits = tile(image_low[...].reshape(3 * rows, depth), text_low[0])
    own_logits = logits[:rows]
    own_coef = (sharp * (jax.nn.sigmoid(own_logits) - same)).astype(BF16)
    all_coef = jnp.concatenate([own_coef, coefs(logits[rows:])], axis=0)
    split_out(back_out, dot(image_turned[...], all_coef, (1, 0)), raw[...])
    back_in[n] = back_out[n]
    each(n_narrow - 1, lambda k: back_copy(peer(k), n).start())

    @pl.when(edge)
    def _():
        def take_across(k):
            p = peer(k)
            edge_copy(p, p).wait_recv()
            unpack(edge_got, edge_raw, p, p)

        each(n_narrow, take_across)
        words = unit_words(edge_raw[...])[0].astype(BF16)
        text_low[across_slot] = words
        part = dot(image_turned[:, :rows], coefs(tile(image_low[0], words)), (1, 0))
        split_out(edge_out, part, edge_raw[...])
        each(n_narrow, lambda k: edge_back_copy(peer(k), n).start())

    losses = softplus((1.0 - 2.0 * same) * own_logits)
    image_sum = dot(own_coef, text_low[0], (1, 1))
    for slot in (1, 2):
        def take_beside():
            for side in range(2):
                text_copy(slot, side).wait_recv()
            each(n_narrow, lambda p: unpack(beside.at[slot - 1], edge_raw, p, spot(p)))
            text_low[slot] = unit_words(edge_raw[...])[0].astype(BF16)

        from_neighbours(slot, take_beside)
        logits = tile(image_low[0], text_low[slot])
        losses = losses + softplus(logits)
        image_sum = image_sum + dot(coefs(logits), text_low[slot], (1, 1))
    loss_ref[...] = jnp.sum(losses.T, axis=0, keepdims=True)
    image_unit = pic_ref[...].astype(F32) * image_scale
    image_inner = jnp.sum(image_unit * image_sum, axis=1, keepdims=True)
    image_grad_ref[...] = (image_sum - image_unit * image_inner) * image_scale

    def block_of(p):
        return (slice(None), pl.ds(pl.multiple_of(p * rows, rows), rows))

    def take_back(k):
        p = peer(k)
        back_copy(p, p).wait_recv()
        text_grad_ref[block_of(p)] = unfold(back_in[p].astype(F32))

    text_grad_ref[block_of(n)] = unfold(back_in[n].astype(F32))
    each(n_narrow - 1, take_back)

    @pl.when(edge)
    def _():
        def take_edge(k):
            p = peer(k)
            edge_back_copy(p, p).wait_recv()
            text_grad_ref[block_of(p)] += unfold(edge_in[p].astype(F32))

        each(n_narrow, take_edge)

    def sent_all(k):
        pack_copy(peer(k), n).wait_send()
        back_copy(peer(k), n).wait_send()

    each(n_narrow - 1, sent_all)

    def sent_whole(slot):
        whole_copy(image_low, image_sent, image_got, slot).wait_send()
        for side in range(2):
            text_copy(slot, side).wait_send()

    to_neighbours(sent_whole)

    @pl.when(edge)
    def _():
        def sent_across(k):
            edge_copy(peer(k), n).wait_send()
            edge_back_copy(peer(k), n).wait_send()

        each(n_narrow, sent_across)


def hand_out(loss, image_grad, text_grad, loss_out, image_out, text_out, sems):
    copies = [
        pltpu.make_async_copy(source, target, sems.at[i])
        for i, (source, target) in enumerate(((text_grad, text_out), (image_grad, image_out), (loss, loss_out)))]
    for copy in copies:
        copy.start()
    for copy in copies:
        copy.wait()


def solution(mesh):
    n_blk, n_narrow = mesh.shape["blk"], mesh.shape["narrow"]

    def step(pictures, captions, sharpness, offset):
        rows, depth = pictures.shape
        words = captions.T
        vmem, smem = pl.BlockSpec(memory_space=pltpu.VMEM), pl.BlockSpec(memory_space=pltpu.SMEM)
        hbm = pl.BlockSpec(memory_space=pltpu.HBM)
        blocks = pltpu.VMEM((n_narrow, 2 * words.shape[0], rows // 2), BF16)
        per_peer, per_side = pltpu.SemaphoreType.DMA((n_narrow,)), pltpu.SemaphoreType.DMA((2,))
        outs = (
            jax.ShapeDtypeStruct((1, rows), F32),
            jax.ShapeDtypeStruct((rows, depth), F32),
            jax.ShapeDtypeStruct(words.shape, F32),
        )
        results = pl.pallas_call(
            functools.partial(kernel, n_blk, n_narrow, RUN),
            out_shape=outs,
            in_specs=[hbm, hbm, smem, smem],
            out_specs=(vmem, vmem, vmem),
            scratch_shapes=[
                pltpu.VMEM(pictures.shape, BF16),
                pltpu.VMEM(words.shape, BF16),
                pltpu.VMEM((3, rows, depth), BF16),
                pltpu.VMEM((depth, 3 * rows), BF16),
                blocks,
                blocks,
                pltpu.VMEM((depth, rows), F32),
                pltpu.VMEM((3, depth, rows), BF16),
                blocks,
                blocks,
                blocks,
                pltpu.VMEM((depth, rows), F32),
                blocks,
                blocks,
                per_side,
                per_peer, per_peer,
                per_side, per_side,
                pltpu.SemaphoreType.DMA((4,)), pltpu.SemaphoreType.DMA((4,)),
                per_peer, per_peer,
                per_peer, per_peer,
                per_peer, per_peer,
                pltpu.VMEM((2, n_narrow, 2 * words.shape[0], rows // 2), BF16),
            ],
            compiler_params=pltpu.CompilerParams(
                collective_id=0, has_side_effects=True, vmem_limit_bytes=48 * 2**20),
        )(*(pltpu.with_memory_space_constraint(x, pltpu.HBM) for x in (pictures, words)), sharpness, offset)
        loss, image_grad, text_grad = pl.pallas_call(
            hand_out,
            out_shape=outs,
            in_specs=[vmem] * 3,
            out_specs=(hbm,) * 3,
            scratch_shapes=[pltpu.SemaphoreType.DMA((3,))],
            compiler_params=pltpu.CompilerParams(vmem_limit_bytes=2**20),
        )(*results)
        return loss.reshape(rows), image_grad, text_grad.T

    return jax.shard_map(
        step,
        mesh=mesh,
        in_specs=(P(("blk", "narrow"), None), P("blk", "narrow"), P(), P()),
        out_specs=(P(("blk", "narrow")), P(("blk", "narrow"), None), P("blk", "narrow")),
        check_vma=False,
    )
```
